512 devices in a mesh: dp: 8 (over x, core), expert: 64 (over y, z).
Axes of the slice: x: 4, y: 4, z: 16, core: 2. Of those that a mesh axis runs over, the one named last changes fastest.
Arguments:
- tokens: bfloat16 [8192, 4096], P('expert', 'dp'), may hold values from -6 to 6
- slot_of: int32 [8192, 8], P('expert'), may hold values from 0 to 95, as said below
- weight_of: float32 [8192, 8], P('expert'), may hold values from 0.05 to 0.5
- gate_up: bfloat16 [64, 2, 4096, 1024], P('expert', None, 'dp')
- down_proj: bfloat16 [64, 1024, 4096], P('expert', None, 'dp')
- spare_up: bfloat16 [64, 2, 4096, 512], P('expert', None, 'dp'), as said below
- spare_down: bfloat16 [64, 1024, 2048], P('expert', None, 'dp'), as said below
Outputs:
- mixed: bfloat16 [8192, 4096], P('expert', 'dp')
The draws below stay inside these ranges and needn't reach their ends.
Inputs may be any that keep to these rules, and one draw needn't show every extreme that they name: `slot_of`: slot e < 64 is expert e's own slot; slot 64 + r is a replica of one of two hot experts, each hot expert having half of the replicas; the 8 entries of a row serve distinct experts. In every aligned block of 128 rows (the rows of one index of expert) no slot serves more than 16 entries and some slot exactly 16, and no expert (own slot and replicas together) is served more than 64 times, some exactly 64 times. spare_up[2 r + h] equals gate_up[e] restricted to hidden units h * 512 to (h + 1) * 512 - 1, for the expert e that slot 64 + r replicates. spare_down[2 r + h] holds the columns of down_proj[e] that the first step assigns to half h, for the expert e that slot 64 + r replicates.
All inputs are finite; a program needn't handle non-finite values.
Results may differ from the reference program's by a relative error of at most 0.029.
Values may be sent and summed in bfloat16 or wider, within the bound.
A program may use at most 128 MiB of HBM per device.

```python
import math
import jax
import jax.numpy as jnp
from jax import lax

D = 4096
FF = 1024
TOPK = 8
ROWS_GRP = 128
TOKENS = 8192
CAP = 16
N_DP = 8
N_EXPERT = 64


def routing_plan(key):
    expert_count = N_EXPERT
    group_count = TOKENS // ROWS_GRP
    half_rows = ROWS_GRP // 2
    cold_count = expert_count - 8
    quarter = expert_count // 4
    slot_most = 7 * ROWS_GRP // cold_count
    top_load = min(slot_most, half_rows)
    key_order, key_spare, key_rows, key_lists, key_turn, key_start = jax.random.split(key, 6)
    expert_order = jax.random.permutation(key_order, expert_count).astype(jnp.int32)
    hot_first = expert_order[0]
    hot_second = expert_order[1]
    steady_expert = expert_order[2]
    other_experts = expert_order[3:]
    spare_rank = jax.random.permutation(key_spare, expert_count // 2).astype(jnp.int32)
    spare_side = (spare_rank >= quarter).astype(jnp.int32)
    spare_expert = jnp.where(spare_side == 0, hot_first, hot_second).astype(jnp.int32)
    side_replicas = jnp.stack([jnp.argsort((spare_side != side_value).astype(jnp.int32), stable=True)[:quarter] for side_value in (0, 1)]).astype(jnp.int32)
    group_keys = jax.random.split(key_rows, group_count)
    row_perm = jax.vmap(lambda group_key: jax.random.permutation(group_key, ROWS_GRP))(group_keys).astype(jnp.int32)
    row_side = (row_perm >= half_rows).astype(jnp.int32)
    hot_rank = row_perm % half_rows
    list_keys = jax.random.split(key_lists, group_count)
    shuffled = jax.vmap(lambda group_key: jax.random.permutation(group_key, other_experts))(list_keys).astype(jnp.int32)
    steady_column = jnp.full((group_count, 1), steady_expert, jnp.int32)
    cold_list = jnp.concatenate([steady_column, shuffled[:, :cold_count - 1]], 1)
    row_index = jnp.arange(ROWS_GRP, dtype=jnp.int32)[:, None]
    cold_pick = (7 * row_index + jnp.arange(TOPK - 1, dtype=jnp.int32)[None, :]) % cold_count
    cold_slots = cold_list[:, cold_pick]
    replica_count = 1 + quarter
    group_index = jnp.arange(group_count, dtype=jnp.int32)[:, None]
    start_shift = jax.random.randint(key_start, (), 0, replica_count).astype(jnp.int32)
    group_offset = (group_index + start_shift) % replica_count
    position = jnp.where(hot_rank < top_load, 0, 1 + jnp.maximum(hot_rank - top_load, 0) % quarter).astype(jnp.int32)
    replica_pick = (position + group_offset) % replica_count
    hot_expert = jnp.where(row_side == 0, hot_first, hot_second)
    spare_replica = side_replicas[row_side, jnp.maximum(replica_pick - 1, 0)]
    hot_slot = jnp.where(replica_pick == 0, hot_expert, expert_count + spare_replica)
    entries = jnp.concatenate([hot_slot[..., None], cold_slots], -1)
    column_turn = jax.random.randint(key_turn, (group_count, ROWS_GRP, 1), 0, TOPK).astype(jnp.int32)
    column_source = (jnp.arange(TOPK, dtype=jnp.int32)[None, None, :] - column_turn) % TOPK
    slot_table = jnp.take_along_axis(entries, column_source, -1)
    return (spare_expert, slot_table.reshape(TOKENS, TOPK).astype(jnp.int32))


def expert_gates(key, expert_ids):
    base = jax.random.fold_in(key, 11)

    def single(expert_id):
        return jax.random.normal(jax.random.fold_in(base, expert_id), (2, D, FF), jnp.float32) * D ** (-0.5)
    return jax.vmap(single)(expert_ids).astype(jnp.bfloat16)


def expert_downs(key, expert_ids):
    base = jax.random.fold_in(key, 12)

    def single(expert_id):
        return jax.random.normal(jax.random.fold_in(base, expert_id), (FF, D), jnp.float32) * FF ** (-0.5)
    return jax.vmap(single)(expert_ids).astype(jnp.bfloat16)


def draw_slot_of(key, part):
    return routing_plan(key)[1]


def draw_gate_up(key, part):
    return expert_gates(key, jnp.arange(N_EXPERT, dtype=jnp.int32))


def draw_down_proj(key, part):
    return expert_downs(key, jnp.arange(N_EXPERT, dtype=jnp.int32))


def draw_spare_up(key, part):
    spare_expert = routing_plan(key)[0]
    whole = expert_gates(key, spare_expert)
    whole = whole.reshape(N_EXPERT // 2, 2, D, 2, FF // 2).transpose(0, 3, 1, 2, 4)
    return whole.reshape(N_EXPERT, 2, D, FF // 2)


def draw_spare_down(key, part):
    spare_expert = routing_plan(key)[0]
    whole = expert_downs(key, spare_expert)
    whole = whole.reshape(N_EXPERT // 2, FF, N_DP, 2, D // N_DP // 2).transpose(0, 3, 1, 2, 4)
    return whole.reshape(N_EXPERT, FF, D // 2)


def block_levels(key, dims, pieces, least, largest):
    level = 1.0
    for dim, parts in pieces:
        steps = jax.random.uniform(jax.random.fold_in(jax.random.fold_in(key, 6), dim), (parts,), jnp.float32, least / len(pieces), largest / len(pieces))
        level = level * jnp.repeat(jnp.exp(steps), dims[dim] // parts).reshape((-1,) + (1,) * (len(dims) - 1 - dim))
    return level


def normal_values(rng, shape, scale, reach, cuts=(), kind=jnp.bfloat16):
    array = jax.random.normal(rng, shape, jnp.float32) * scale
    if len(cuts) > 0:
        array = block_levels(rng, shape, cuts, -0.22, 0.18) * array
    return jnp.clip(array, min=-reach, max=reach).astype(kind)


def setup_inputs(seed: int = 0) -> dict:
    streams_of = jax.random.split(jax.random.key(seed), 8)
    return {
        "tokens": normal_values(streams_of[0], (TOKENS, D), 1.0, 6.0, ((0, 64), (1, 8))),
        "slot_of": draw_slot_of(jax.random.fold_in(streams_of[7], 71), 0),
        "weight_of": jnp.clip(jnp.exp(math.log(0.5) - 2.3025851 * jax.random.uniform(streams_of[2], (TOKENS, TOPK), jnp.float32) ** block_levels(streams_of[2], (TOKENS, TOPK), ((0, 64),), -0.2, 0.2)), 0.05, 0.5),
        "gate_up": draw_gate_up(jax.random.fold_in(streams_of[7], 71), 0),
        "down_proj": draw_down_proj(jax.random.fold_in(streams_of[7], 71), 0),
        "spare_up": draw_spare_up(jax.random.fold_in(streams_of[7], 71), 0),
        "spare_down": draw_spare_down(jax.random.fold_in(streams_of[7], 71), 0),
    }


def reference(tokens, slot_of, weight_of, gate_up, down_proj, spare_up, spare_down):
    assign_count = TOKENS * TOPK
    flat_slot = slot_of.reshape(assign_count)
    flat_weight = weight_of.reshape(assign_count)
    buffer_rows = CAP * N_EXPERT
    slice_width = D // N_DP
    half_slice = slice_width // 2

    def pick_rows(slot_id):
        picked = jnp.nonzero(flat_slot == slot_id, size=buffer_rows, fill_value=assign_count)[0].astype(jnp.int32)
        is_live = picked < assign_count
        row_ids = jnp.where(is_live, picked // TOPK, 0).astype(jnp.int32)
        safe_pick = jnp.minimum(picked, assign_count - 1)
        row_weight = jnp.where(is_live, flat_weight[safe_pick], jnp.float32(0.0))
        return row_ids, row_weight

    def hidden_of(chosen, expert_up):
        width = expert_up.shape[2]
        summed = jnp.zeros((buffer_rows, 2, width), jnp.float32)
        for slice_index in range(N_DP):
            low = slice_index * slice_width
            left = chosen[:, low:low + slice_width].astype(jnp.float32)
            right = expert_up[:, low:low + slice_width, :].astype(jnp.float32)
            partial_sum = jnp.einsum("rd,qdf->rqf", left, right)
            rounded = lax.optimization_barrier(partial_sum.astype(jnp.bfloat16))
            summed = summed + rounded.astype(jnp.float32)
        return (jax.nn.silu(summed[:, 0, :]) * summed[:, 1, :]).astype(jnp.bfloat16)

    def own_step(accum, slot_id):
        row_ids, row_weight = pick_rows(slot_id)
        hidden = hidden_of(tokens[row_ids], gate_up[slot_id])
        expert_out = jnp.dot(hidden, down_proj[slot_id], preferred_element_type=jnp.float32)
        expert_out = lax.optimization_barrier(expert_out.astype(jnp.bfloat16))
        accum = accum.at[row_ids].add(row_weight[:, None] * expert_out.astype(jnp.float32))
        return accum, None

    def spare_step(accum, rep_id):
        row_ids, row_weight = pick_rows(N_EXPERT + rep_id)
        chosen = tokens[row_ids]
        halves = [hidden_of(chosen, spare_up[2 * rep_id + half]) for half in range(2)]
        hidden = jnp.concatenate(halves, 1)
        outs = [jnp.dot(hidden, spare_down[2 * rep_id + half], preferred_element_type=jnp.float32) for half in range(2)]
        stacked = jnp.stack(outs, 1).reshape(buffer_rows, 2, N_DP, half_slice)
        expert_out = stacked.transpose(0, 2, 1, 3).reshape(buffer_rows, D)
        expert_out = lax.optimization_barrier(expert_out.astype(jnp.bfloat16))
        accum = accum.at[row_ids].add(row_weight[:, None] * expert_out.astype(jnp.float32))
        return accum, None

    start = jnp.zeros((TOKENS, D), jnp.float32)
    accum, _ = lax.scan(own_step, start, jnp.arange(N_EXPERT, dtype=jnp.int32))
    accum, _ = lax.scan(spare_step, accum, jnp.arange(N_EXPERT // 2, dtype=jnp.int32))
    return accum.astype(jnp.bfloat16)
```

```python
import jax
import jax.numpy as jnp
from jax import lax
from jax.experimental import pallas as pl
from jax.experimental.pallas import tpu as pltpu
from jax.sharding import PartitionSpec as P

NX, NY, NZ = 4, 4, 16
CAP = 16
BF = jnp.bfloat16
F32 = jnp.float32
MESH = pl.DeviceIdType.MESH
UNITS = NZ // 2
STAGE0 = 4
STEPS = UNITS + STAGE0 + 9


def mod(value, n):
    return lax.rem(value, n)


def kernel(
    tok_ref, meta_ref, gate_ref, down_ref, sup_ref, sdown_ref, out_ref,
    wall, wd, wsd, tok_all, meta_all, sel, arr, part, crecv, qbuf, rhalf, rfull, hid, outs,
    rland, oland, back, dense, zsend, zland,
    w_sem, z_s, z_r, m_s, m_r, y_s, y_r, yr_s, yr_r, c_s, c_r, xa_s, xa_r, xb_s, xb_r, p_s, p_r,
    g_s, g_r, h_s, h_r, ch_s, ch_r, o_s, o_r, or_s, or_r, zz_s, zz_r,
):
    dp = lax.axis_index("dp")
    ex = lax.axis_index("expert")
    x, c = dp // 2, mod(dp, 2)
    y, z = ex // NZ, mod(ex, NZ)
    half = mod(z, 2)
    pair = z // 2
    x1, x2, x3 = mod(x + 1, NX), mod(x + 2, NX), mod(x + 3, NX)
    y1, y2, y3 = mod(y + 1, NY), mod(y + 2, NY), mod(y + 3, NY)
    z1, z3 = mod(z + 1, NZ), mod(z + NZ - 1, NZ)
    dev_xp, dev_xm = (x1 * 2 + c, ex), (x3 * 2 + c, ex)
    dev_c = (x * 2 + (1 - c), ex)
    dev_yp, dev_ym = (dp, y1 * NZ + z), (dp, y3 * NZ + z)
    dev_zp, dev_zm = (dp, y * NZ + z1), (dp, y * NZ + z3)
    dev_pt = (dp, y * NZ + pair * 2 + (1 - half))

    def rc(src, dst, ssem, rsem, dev):
        return pltpu.make_async_remote_copy(
            src_ref=src, dst_ref=dst, send_sem=ssem, recv_sem=rsem, device_id=dev, device_id_type=MESH
        )

    loads = [
        pltpu.make_async_copy(gate_ref.at[0, 0], wall.at[:, 0:1024], w_sem.at[0]),
        pltpu.make_async_copy(gate_ref.at[0, 1], wall.at[:, 1024:2048], w_sem.at[1]),
        pltpu.make_async_copy(sup_ref.at[0, 0], wall.at[:, 2048:2560], w_sem.at[2]),
        pltpu.make_async_copy(sup_ref.at[0, 1], wall.at[:, 2560:3072], w_sem.at[3]),
        pltpu.make_async_copy(down_ref.at[0], wd, w_sem.at[4]),
        pltpu.make_async_copy(sdown_ref.at[0], wsd, w_sem.at[5]),
    ]
    for load in loads:
        load.start()

    tok_all[z] = tok_ref[...]
    meta_all[z] = meta_ref[...]

    barrier = pltpu.get_barrier_semaphore()
    for dev in (dev_xp, dev_xm, dev_c, dev_yp, dev_ym, dev_zp, dev_zm):
        pl.semaphore_signal(barrier, inc=1, device_id=dev, device_id_type=MESH)
    pl.semaphore_wait(barrier, 7)

    def z_block(d, i):
        return mod(z + NZ - i, NZ) if d == 0 else mod(z + i, NZ)

    def z_copy(d, i, k, block):
        piece = tok_all.at[block, 64 * k:64 * k + 64]
        return rc(piece, piece, z_s.at[d, i, k], z_r.at[d, i, k], dev_zp if d == 0 else dev_zm)

    def m_copy(d, i, block):
        piece = meta_all.at[block]
        return rc(piece, piece, m_s.at[d, i], m_r.at[d, i], dev_zp if d == 0 else dev_zm)

    def hop_send(d, i, k):
        z_copy(d, i, k, z_block(d, i)).start()

    def hop_wait(d, i, k):
        z_copy(d, i, k, z_block(d, i + 1)).wait_recv()

    for d in (0, 1):
        m_copy(d, 0, z_block(d, 0)).start()
    for k in (0, 1):
        for d in (0, 1):
            hop_send(d, 0, k)

    group = lax.broadcasted_iota(jnp.int32, (8, 128), 0)
    tri = (
        lax.broadcasted_iota(jnp.int32, (128, 128), 0) < lax.broadcasted_iota(jnp.int32, (128, 128), 1)
    ).astype(BF)
    place = lax.broadcasted_iota(jnp.int32, (8, CAP, 128), 1).astype(F32)

    def slot_ids(row, spare):
        own = row * NZ + z
        return jnp.where(spare == 1, NY * NZ + own // 2, own).astype(F32)

    send_ids = slot_ids(mod(y + group // 2 + 1, NY), mod(group, 2))
    back_ids = slot_ids(mod(group, 4), group // 4)

    def codes(meta, ids):
        mask = jnp.zeros((8, 128), F32)
        for k in range(8):
            mask = mask + jnp.where(meta[k:k + 1, :] == ids, 1.0, 0.0)
        rank = jnp.dot(mask.astype(BF), tri, preferred_element_type=F32)
        code = jnp.where(mask > 0.5, rank, -1.0)
        return jnp.broadcast_to(code[:, None, :], (8, CAP, 128)) == place

    def y_copy(block, n):
        if n == 0:
            return rc(sel.at[block, 0:32], arr.at[block, y], y_s.at[block, 0], y_r.at[block, 0], dev_yp)
        if n == 1:
            return rc(sel.at[block, 64:96], arr.at[block, y], y_s.at[block, 1], y_r.at[block, 1], dev_ym)
        if n == 2:
            return rc(sel.at[block, 32:48], rland.at[block, 0], y_s.at[block, 2], y_r.at[block, 2], dev_yp)
        return rc(sel.at[block, 48:64], rland.at[block, 1], y_s.at[block, 3], y_r.at[block, 3], dev_ym)

    def yr_copy(block, n):
        if n == 0:
            return rc(rland.at[block, 0], arr.at[block, y3, 0:16], yr_s.at[block, 0], yr_r.at[block, 0], dev_yp)
        return rc(rland.at[block, 1], arr.at[block, y1, 16:32], yr_s.at[block, 1], yr_r.at[block, 1], dev_ym)

    def select(block):
        hot = codes(meta_all[block], send_ids)
        pick = jnp.where(hot, 1.0, 0.0).astype(BF).reshape(128, 128)
        rows = jnp.dot(pick, tok_all[block], preferred_element_type=F32).astype(BF)
        sel[block] = rows
        for n in (2, 3, 0, 1):
            y_copy(block, n).start()
        arr[block, y] = rows[96:128]

    def relay(block):
        y_copy(block, 2).wait_recv()
        yr_copy(block, 0).start()
        y_copy(block, 3).wait_recv()
        yr_copy(block, 1).start()

    def arrivals(block):
        y_copy(block, 0).wait_recv()
        y_copy(block, 1).wait_recv()
        yr_copy(block, 0).wait_recv()
        yr_copy(block, 1).wait_recv()

    def unit_of(u):
        sign = 2 * mod(u, 2) - 1
        return mod(pair + ((u + 1) // 2) * sign + UNITS, UNITS)

    def c_copy(u):
        return rc(part.at[u, 1 - c], crecv.at[u], c_s.at[u], c_r.at[u], dev_c)

    def xa_copy(u, n):
        if n == 0:
            return rc(qbuf.at[u, x2, :, 0:1536], rhalf.at[u, 0], xa_s.at[u, 0], xa_r.at[u, 0], dev_xp)
        return rc(qbuf.at[u, x2, :, 1536:3072], rhalf.at[u, 1], xa_s.at[u, 1], xa_r.at[u, 1], dev_xm)

    def xb_copy(u, n):
        if n == 0:
            return rc(qbuf.at[u, x1], rfull.at[u, 0], xb_s.at[u, 0], xb_r.at[u, 0], dev_xp)
        return rc(qbuf.at[u, x3], rfull.at[u, 1], xb_s.at[u, 1], xb_r.at[u, 1], dev_xm)

    def p_copy(u):
        piece = hid.at[u, c, x, :, pl.ds(pl.multiple_of(1024 + half * 512, 512), 512)]
        return rc(piece, piece, p_s.at[u], p_r.at[u], dev_pt)

    def g_copy(u, n):
        piece = hid.at[u, c, x]
        return rc(piece, piece, g_s.at[u, n], g_r.at[u, n], dev_xp if n == 0 else dev_xm)

    def h_copy(u, n):
        if n == 0:
            piece = hid.at[u, c, x3, :, 0:1024]
            return rc(piece, piece, h_s.at[u, 0], h_r.at[u, 0], dev_xp)
        piece = hid.at[u, c, x1, :, 1024:2048]
        return rc(piece, piece, h_s.at[u, 1], h_r.at[u, 1], dev_xm)

    def ch_copy(u):
        piece = hid.at[u, c]
        return rc(piece, piece, ch_s.at[u], ch_r.at[u], dev_c)

    def o_copy(u, n):
        if n == 0:
            return rc(outs.at[u, y1], back.at[u, y], o_s.at[u, 0], o_r.at[u, 0], dev_yp)
        if n == 1:
            return rc(outs.at[u, y3], back.at[u, y], o_s.at[u, 1], o_r.at[u, 1], dev_ym)
        if n == 2:
            return rc(
                outs.at[u, y2, :, :, 0:384], oland.at[u, 0], o_s.at[u, 2], o_r.at[u, 2], dev_yp
            )
        return rc(
            outs.at[u, y2, :, :, 384:768], oland.at[u, 1], o_s.at[u, 3], o_r.at[u, 3], dev_ym
        )

    def or_copy(u, n):
        if n == 0:
            return rc(
                oland.at[u, 0], back.at[u, y3, :, :, 0:384], or_s.at[u, 0], or_r.at[u, 0], dev_yp
            )
        return rc(
            oland.at[u, 1], back.at[u, y1, :, :, 384:768], or_s.at[u, 1], or_r.at[u, 1], dev_ym
        )

    def multiply_up(u):
        @pl.when(u == 0)
        def _():
            for load in loads[:4]:
                load.wait()

        q = unit_of(u)
        arrivals(2 * q)
        arrivals(2 * q + 1)
        own = arr[pl.ds(2 * q, 2), :, 0:16, :].reshape(128, 512)
        spare = arr[pl.ds(2 * q, 2), :, 16:32, :].reshape(128, 512)
        for n in range(6):
            cols = slice(512 * n, 512 * n + 512)
            made = jnp.dot(own if n < 4 else spare, wall[:, cols], preferred_element_type=F32)
            part[u, :, :, :, cols] = made.astype(BF).reshape(2, 4, 16, 512)
        c_copy(u).start()

    def add_core(u):
        c_copy(u).wait_recv()
        for n, row in enumerate((x2, x1, x3, x)):
            qbuf[u, row] = (part[u, c, row].astype(F32) + crecv[u, row].astype(F32)).astype(BF)
            if n == 0:
                xa_copy(u, 0).start()
                xa_copy(u, 1).start()

    def add_far(u):
        for n, row, cols in ((0, x1, slice(0, 1536)), (1, x3, slice(1536, 3072))):
            xa_copy(u, n).wait_recv()
            both = qbuf[u, row, :, cols].astype(F32) + rhalf[u, n].astype(F32)
            qbuf[u, row, :, cols] = both.astype(BF)
            xb_copy(u, n).start()

    def activate(u):
        xb_copy(u, 0).wait_recv()
        xb_copy(u, 1).wait_recv()

        def total(low, width):
            cols = slice(low, low + width)
            mine = qbuf[u, x, :, cols].astype(F32)
            return mine + rfull[u, 0, :, cols].astype(F32) + rfull[u, 1, :, cols].astype(F32)

        def silu_product(low, width):
            gate = total(low, width)
            return (gate / (1.0 + jnp.exp(-gate)) * total(low + width, width)).astype(BF)

        at = pl.ds(pl.multiple_of(1024 + half * 512, 512), 512)
        hid[u, c, x, :, at] = silu_product(2048, 512)
        p_copy(u).start()
        hid[u, c, x, :, 0:1024] = silu_product(0, 1024)

    def gather_near(u):
        p_copy(u).wait_recv()
        g_copy(u, 0).start()
        g_copy(u, 1).start()

    def gather_far(u):
        for n in (0, 1):
            g_copy(u, n).wait_recv()
            h_copy(u, n).start()

    def gather_core(u):
        h_copy(u, 0).wait_recv()
        h_copy(u, 1).wait_recv()
        ch_copy(u).start()

    def multiply_down(u):
        @pl.when(u == 0)
        def _():
            for load in loads[4:]:
                load.wait()

        ch_copy(u).wait_recv()
        own = hid[u, :, :, :, 0:1024].reshape(128, 1024)
        spare = hid[u, :, :, :, 1024:2048].reshape(128, 1024)
        own_out = jnp.dot(own, wd[...], preferred_element_type=F32).astype(BF).reshape(2, 4, 16, 512)
        spare_out = jnp.dot(spare, wsd[...], preferred_element_type=F32).astype(BF).reshape(2, 4, 16, 256)
        for p in (0, 1):
            outs[u, :, p, :, 0:512] = own_out[p]
            outs[u, :, p, :, 512:768] = spare_out[p]
        for n in (2, 3, 0, 1):
            o_copy(u, n).start()
        back[u, y] = outs[u, y]

    def relay_back(u):
        for n in (0, 1):
            o_copy(u, 2 + n).wait_recv()
            or_copy(u, n).start()

    def combine(u):
        for n in (0, 1):
            o_copy(u, n).wait_recv()
            or_copy(u, n).wait_recv()
        q = unit_of(u)
        at = pl.ds(pl.multiple_of(half * 256, 256), 256)
        for p in (0, 1):
            block = 2 * q + p
            meta = meta_all[block]
            share = jnp.zeros((8, 128), F32)
            for k in range(8):
                share = share + jnp.where(meta[k:k + 1, :] == back_ids, meta[8 + k:9 + k, :], 0.0)
            spread = jnp.broadcast_to(share[:, None, :], (8, CAP, 128))
            weight = jnp.where(codes(meta, back_ids), spread, 0.0).astype(BF).reshape(128, 128)
            own = back[u, :, p, :, 0:512].reshape(64, 512)
            spare = back[u, :, p, :, 512:768].reshape(64, 256)
            over = (((0,), (0,)), ((), ()))
            dense[block] = lax.dot_general(weight[0:64], own, over, preferred_element_type=F32)
            more = lax.dot_general(weight[64:128], spare, over, preferred_element_type=F32)
            dense[block, :, at] = dense[block, :, at] + more

    def hops(t):
        @pl.when((t >= 1) & (t <= 7))
        def _():
            for d in (0, 1):
                m_copy(d, t - 1, z_block(d, t)).wait_recv()
            m_copy(0, t, z_block(0, t)).start()

            @pl.when(t <= 6)
            def _():
                m_copy(1, t, z_block(1, t)).start()

            for k in (0, 1):
                for d in (0, 1):
                    hop_wait(d, t - 1, k)
                    if k == d:
                        hop_send(d, t, k)
                    else:
                        @pl.when(t <= 6)
                        def _():
                            hop_send(d, t, k)

        @pl.when(t == 8)
        def _():
            m_copy(0, 7, z_block(0, 8)).wait_recv()
            hop_wait(0, 7, 0)
            hop_wait(1, 7, 1)

    stages = [
        (4 + 9, combine), (4 + 8, relay_back), (4 + 6, gather_core), (4 + 5, gather_far),
        (4 + 4, gather_near), (4 + 3, activate), (4 + 2, add_far), (4 + 1, add_core),
        (4 + 7, multiply_down), (4, multiply_up),
    ]

    def step(t, carry):
        hops(t)

        @pl.when((t >= 1) & (t <= 9))
        def _():
            relay(z_block(0, t - 1))

        @pl.when((t >= 2) & (t <= 8))
        def _():
            relay(z_block(1, t - 1))

        for offset, stage in stages:
            @pl.when((t >= offset) & (t < offset + UNITS))
            def _():
                stage(t - offset)

        @pl.when(t <= 8)
        def _():
            select(z_block(0, t))

        @pl.when((t >= 1) & (t <= 7))
        def _():
            select(z_block(1, t))

        return carry

    lax.fori_loop(0, STEPS, step, 0)

    def zz_copy(d, j, k):
        rows = slice(64 * k, 64 * k + 64)
        return rc(
            zsend.at[d, j, rows], zland.at[d, j, rows], zz_s.at[d, j, k], zz_r.at[d, j, k],
            dev_zm if d == 0 else dev_zp,
        )

    def chain(j, first, second):
        for k in (0, 1):
            rows = slice(64 * k, 64 * k + 64)
            for d in (0, 1):
                if first and k != d:
                    continue
                block = mod(z + NZ - 8 + j, NZ) if d == 0 else mod(z + 8 - j, NZ)
                value = dense[block, rows]
                if not first and not (second and k != d):
                    zz_copy(d, j - 1, k).wait_recv()
                    value = value + zland[d, j - 1, rows].astype(F32)
                zsend[d, j, rows] = value.astype(BF)
                zz_copy(d, j, k).start()

    chain(0, True, False)
    chain(1, False, True)

    def chain_step(j, carry):
        chain(j, False, False)
        return carry

    lax.fori_loop(2, 8, chain_step, 0)
    for k in (0, 1):
        rows = slice(64 * k, 64 * k + 64)
        for d in (0, 1):
            zz_copy(d, 7, k).wait_recv()
        value = dense[z, rows] + zland[0, 7, rows].astype(F32) + zland[1, 7, rows].astype(F32)
        out_ref[rows] = value.astype(BF)

    def drain_hops(i, carry):
        m_copy(0, i, z_block(0, i)).wait_send()
        for d in (0, 1):
            z_copy(d, i, d, z_block(d, i)).wait_send()
            zz_copy(d, i, d).wait_send()

        @pl.when(i <= 6)
        def _():
            m_copy(1, i, z_block(1, i)).wait_send()
            for d in (0, 1):
                z_copy(d, i, 1 - d, z_block(d, i)).wait_send()
                zz_copy(d, i + 1, 1 - d).wait_send()

        return carry

    lax.fori_loop(0, 8, drain_hops, 0)

    def drain_blocks(block, carry):
        for n in range(4):
            y_copy(block, n).wait_send()
        for n in range(2):
            yr_copy(block, n).wait_send()
        return carry

    lax.fori_loop(0, NZ, drain_blocks, 0)

    def drain_units(u, carry):
        c_copy(u).wait_send()
        p_copy(u).wait_send()
        ch_copy(u).wait_send()
        for n in range(2):
            for copy in (xa_copy, xb_copy, g_copy, h_copy, or_copy):
                copy(u, n).wait_send()
        for n in range(4):
            o_copy(u, n).wait_send()
        return carry

    lax.fori_loop(0, UNITS, drain_units, 0)


def on_device(tokens, slot_of, weight_of, gate_up, down_proj, spare_up, spare_down):
    meta = jnp.concatenate([slot_of.T.astype(F32), weight_of.T], 0)
    vmem = pl.BlockSpec(memory_space=pltpu.VMEM)
    hbm = pl.BlockSpec(memory_space=pl.ANY)
    dma = pltpu.SemaphoreType.DMA
    return pl.pallas_call(
        kernel,
        out_shape=jax.ShapeDtypeStruct((128, 512), BF),
        in_specs=[vmem, vmem, hbm, hbm, hbm, hbm],
        out_specs=vmem,
        scratch_shapes=[
            pltpu.VMEM((512, 3072), BF),
            pltpu.VMEM((1024, 512), BF),
            pltpu.VMEM((1024, 256), BF),
            pltpu.VMEM((NZ, 128, 512), BF),
            pltpu.VMEM((NZ, 16, 128), F32),
            pltpu.VMEM((NZ, 128, 512), BF),
            pltpu.VMEM((NZ, NY, 32, 512), BF),
            pltpu.VMEM((UNITS, 2, 4, 16, 3072), BF),
            pltpu.VMEM((UNITS, 4, 16, 3072), BF),
            pltpu.VMEM((UNITS, 4, 16, 3072), BF),
            pltpu.VMEM((UNITS, 2, 16, 1536), BF),
            pltpu.VMEM((UNITS, 2, 16, 3072), BF),
            pltpu.VMEM((UNITS, 2, 4, 16, 2048), BF),
            pltpu.VMEM((UNITS, 4, 2, 16, 768), BF),
            pltpu.VMEM((NZ, 2, 16, 512), BF),
            pltpu.VMEM((UNITS, 2, 2, 16, 384), BF),
            pltpu.VMEM((UNITS, 4, 2, 16, 768), BF),
            pltpu.VMEM((NZ, 128, 512), F32),
            pltpu.VMEM((2, 8, 128, 512), BF),
            pltpu.VMEM((2, 8, 128, 512), BF),
            dma((6,)),
            dma((2, 8, 2)), dma((2, 8, 2)),
            dma((2, 8)), dma((2, 8)),
            dma((NZ, 4)), dma((NZ, 4)),
            dma((NZ, 2)), dma((NZ, 2)),
            dma((UNITS,)), dma((UNITS,)),
            dma((UNITS, 2)), dma((UNITS, 2)),
            dma((UNITS, 2)), dma((UNITS, 2)),
            dma((UNITS,)), dma((UNITS,)),
            dma((UNITS, 2)), dma((UNITS, 2)),
            dma((UNITS, 2)), dma((UNITS, 2)),
            dma((UNITS,)), dma((UNITS,)),
            dma((UNITS, 4)), dma((UNITS, 4)),
            dma((UNITS, 2)), dma((UNITS, 2)),
            dma((2, 8, 2)), dma((2, 8, 2)),
        ],
        compiler_params=pltpu.CompilerParams(
            collective_id=0, has_side_effects=True, vmem_limit_bytes=58 * 1024 * 1024
        ),
        cost_estimate=pl.CostEstimate(flops=5 * 10**9, bytes_accessed=6 * 10**6, transcendentals=10**5),
    )(tokens, meta, gate_up, down_proj, spare_up, spare_down)


def solution(mesh):
    in_specs = (
        P("expert", "dp"),
        P("expert", None),
        P("expert", None),
        P("expert", None, "dp", None),
        P("expert", None, "dp"),
        P("expert", None, "dp", None),
        P("expert", None, "dp"),
    )
    out_specs = P("expert", "dp")
    return jax.shard_map(
        on_device, mesh=mesh, in_specs=in_specs, out_specs=out_specs, check_vma=False
    )
```

```python
import jax
import jax.numpy as jnp
from jax import lax
from jax.experimental import pallas as pl
from jax.experimental.pallas import tpu as pltpu
from jax.sharding import PartitionSpec as P

NX, NY, NZ = 4, 4, 16
CAP = 16
BF = jnp.bfloat16
F32 = jnp.float32
MESH = pl.DeviceIdType.MESH
UNITS = NZ // 2
STEPS = UNITS + 10
DEEP = 4
PIECES = 8
PIECE = 128 // PIECES


def mod(value, n):
    return lax.rem(value, n)


def kernel(
    tok_ref, slot_ref, weight_ref, gate_ref, down_ref, sup_ref, sdown_ref, out_ref,
    wall, wd, wsd, tok_all, meta_all, sel, arr, part, crecv, qbuf, rhalf, rfull, hid, hother, outs,
    back, dense, zsend, zland,
    w_sem, z_s, z_r, m_s, m_r, y_s, y_r, c_s, c_r, xa_s, xa_r, xb_s, xb_r,
    g_s, g_r, h_s, h_r, ch_s, ch_r, o_s, o_r, zz_s, zz_r,
):
    dp = lax.axis_index("dp")
    ex = lax.axis_index("expert")
    x, c = dp // 2, mod(dp, 2)
    y, z = ex // NZ, mod(ex, NZ)
    half = mod(z, 2)
    pair = z // 2
    x1, x2, x3 = mod(x + 1, NX), mod(x + 2, NX), mod(x + 3, NX)
    y1, y2, y3 = mod(y + 1, NY), mod(y + 2, NY), mod(y + 3, NY)
    z1, z3 = mod(z + 1, NZ), mod(z + NZ - 1, NZ)
    dev_xp, dev_xm = (x1 * 2 + c, ex), (x3 * 2 + c, ex)
    dev_c = (x * 2 + (1 - c), ex)
    dev_zp, dev_zm = (dp, y * NZ + z1), (dp, y * NZ + z3)
    mate = y * NZ + pair * 2 + (1 - half)
    dev_pt, dev_ptc = (dp, mate), (x * 2 + (1 - c), mate)
    dev_y = [(dp, row * NZ + z) for row in (y1, y2, y3)]

    def rc(src, dst, ssem, rsem, dev):
        return pltpu.make_async_remote_copy(
            src_ref=src, dst_ref=dst, send_sem=ssem, recv_sem=rsem, device_id=dev, device_id_type=MESH
        )

    loads = [
        pltpu.make_async_copy(gate_ref.at[0, 0], wall.at[:, 0:1024], w_sem.at[0]),
        pltpu.make_async_copy(gate_ref.at[0, 1], wall.at[:, 1024:2048], w_sem.at[1]),
        pltpu.make_async_copy(sup_ref.at[0, 0], wall.at[:, 2048:2560], w_sem.at[2]),
        pltpu.make_async_copy(sup_ref.at[0, 1], wall.at[:, 2560:3072], w_sem.at[3]),
        pltpu.make_async_copy(down_ref.at[0], wd, w_sem.at[4]),
        pltpu.make_async_copy(sdown_ref.at[0], wsd, w_sem.at[5]),
    ]
    for load in loads:
        load.start()

    tok_all[z] = tok_ref[...]
    meta_all[z, 0:8] = slot_ref[...].astype(F32)
    meta_all[z, 8:16] = weight_ref[...]

    barrier = pltpu.get_barrier_semaphore()
    for dev in (dev_xp, dev_xm, dev_c, dev_zp, dev_zm, dev_ptc, *dev_y):
        pl.semaphore_signal(barrier, inc=1, device_id=dev, device_id_type=MESH)
    pl.semaphore_wait(barrier, 9)

    def z_block(d, i):
        return mod(z + NZ - i, NZ) if d == 0 else mod(z + i, NZ)

    def z_copy(d, i, k, block):
        piece = tok_all.at[block, PIECE * k:PIECE * k + PIECE]
        at = (d, mod(i, 2), k)
        return rc(piece, piece, z_s.at[at], z_r.at[at], dev_zp if d == 0 else dev_zm)

    def m_copy(d, i, block):
        piece = meta_all.at[block]
        at = (d, mod(i, 2))
        return rc(piece, piece, m_s.at[at], m_r.at[at], dev_zp if d == 0 else dev_zm)

    def hop_send(d, i, k):
        z_copy(d, i, k, z_block(d, i)).start()

    def hop_left(d, i, k):
        z_copy(d, i, k, z_block(d, i)).wait_send()

    def hop_wait(d, i, k):
        z_copy(d, i, k, z_block(d, i + 1)).wait_recv()

    group = lax.broadcasted_iota(jnp.int32, (8, 128), 0)
    tri = (
        lax.broadcasted_iota(jnp.int32, (128, 128), 0) < lax.broadcasted_iota(jnp.int32, (128, 128), 1)
    ).astype(BF)
    place = lax.broadcasted_iota(jnp.int32, (8, CAP, 128), 1).astype(F32)

    def slot_ids(row, spare):
        own = row * NZ + z
        return jnp.where(spare == 1, NY * NZ + own // 2, own).astype(F32)

    send_ids = slot_ids(mod(y + group // 2 + 1, NY), mod(group, 2))
    back_ids = slot_ids(mod(group, 4), group // 4)

    def codes(meta, ids):
        mask = jnp.zeros((8, 128), F32)
        for k in range(8):
            mask = mask + jnp.where(meta[k:k + 1, :] == ids, 1.0, 0.0)
        rank = jnp.dot(mask.astype(BF), tri, preferred_element_type=F32)
        code = jnp.where(mask > 0.5, rank, -1.0)
        return jnp.broadcast_to(code[:, None, :], (8, CAP, 128)) == place

    def y_copy(d, h, block, n):
        at = (d, mod(h, DEEP), n)
        return rc(sel.at[block, 32 * n:32 * n + 32], arr.at[block, y], y_s.at[at], y_r.at[at], dev_y[n])

    def select_one(d, h):
        block = z_block(d, h)

        @pl.when(h >= DEEP + d)
        def _():
            for n in range(3):
                y_copy(d, h - DEEP, z_block(d, h - DEEP), n).wait_send()

        hot = codes(meta_all[block], send_ids)
        pick = jnp.where(hot, 1.0, 0.0).astype(BF).reshape(128, 128)
        rows = jnp.dot(pick, tok_all[block], preferred_element_type=F32).astype(BF)
        sel[block] = rows
        for n in range(3):
            y_copy(d, h, block, n).start()
        arr[block, y] = rows[96:128]

    def select(h):
        select_one(0, h)

        @pl.when((h >= 1) & (h <= 7))
        def _():
            select_one(1, h)

    def arrive(h):
        for n in range(3):
            y_copy(0, h, z_block(0, h), n).wait_recv()

        @pl.when((h >= 1) & (h <= 7))
        def _():
            for n in range(3):
                y_copy(1, h, z_block(1, h), n).wait_recv()

    def unit_of(u):
        near = jnp.where(u == 0, 0, jnp.where(u == 1, 1, jnp.where(u == 2, UNITS - 1, 2)))
        far = jnp.where(u == 4, 3, jnp.where(u == 5, 4, jnp.where(u == 6, UNITS - 3, UNITS - 2)))
        return mod(pair + jnp.where(u < 4, near, far), UNITS)

    def go(copy, u, n):
        @pl.when(u >= DEEP)
        def _():
            copy(u - DEEP, n).wait_send()

        copy(u, n).start()

    def c_copy(u, n):
        at = mod(u, DEEP)
        return rc(part.at[u, 1 - c], crecv.at[u], c_s.at[at], c_r.at[at], dev_c)

    def xa_copy(u, n):
        at = (mod(u, DEEP), n)
        cols = slice(1536 * n, 1536 * n + 1536)
        return rc(
            qbuf.at[u, x2, :, cols], rhalf.at[u, n], xa_s.at[at], xa_r.at[at], dev_xp if n == 0 else dev_xm
        )

    def xb_copy(u, n):
        at = (mod(u, DEEP), n)
        return rc(
            qbuf.at[u, x1 if n == 0 else x3], rfull.at[u, n], xb_s.at[at], xb_r.at[at],
            dev_xp if n == 0 else dev_xm,
        )

    def g_copy(u, n):
        at = (mod(u, DEEP), n)
        piece = hid.at[u, c, x]
        return rc(piece, piece, g_s.at[at], g_r.at[at], dev_xp if n == 0 else dev_xm)

    def h_copy(u, n):
        at = (mod(u, DEEP), n)
        piece = hid.at[u, c, x3 if n == 0 else x1, :, 768 * n:768 * n + 768]
        return rc(piece, piece, h_s.at[at], h_r.at[at], dev_xp if n == 0 else dev_xm)

    def ch_copy(u, n, rows):
        at = (mod(u, DEEP), n)
        if n == 0:
            piece = hid.at[u, c, rows]
            return rc(piece, piece, ch_s.at[at], ch_r.at[at], dev_c)
        return rc(
            hid.at[u, c, rows, :, 1024:1536], hother.at[u, c, rows], ch_s.at[at], ch_r.at[at],
            dev_pt if n == 1 else dev_ptc,
        )

    def ch_send(u, row):
        for n in (1, 2, 0):
            ch_copy(u, n, row).start()

    def o_copy(u, n):
        at = (mod(u, DEEP), n)
        return rc(outs.at[u, (y1, y2, y3)[n]], back.at[u, y], o_s.at[at], o_r.at[at], dev_y[n])

    def multiply_up(u):
        @pl.when(u == 0)
        def _():
            for load in loads[:4]:
                load.wait()

        q = unit_of(u)
        own = arr[pl.ds(2 * q, 2), :, 0:16, :].reshape(128, 512)
        spare = arr[pl.ds(2 * q, 2), :, 16:32, :].reshape(128, 512)
        for n in range(6):
            cols = slice(512 * n, 512 * n + 512)
            made = jnp.dot(own if n < 4 else spare, wall[:, cols], preferred_element_type=F32)
            part[u, :, :, :, cols] = made.astype(BF).reshape(2, 4, 16, 512)
        go(c_copy, u, 0)

    def add_core(u):
        c_copy(u, 0).wait_recv()
        for n, row in enumerate((x2, x1, x3, x)):
            qbuf[u, row] = (part[u, c, row].astype(F32) + crecv[u, row].astype(F32)).astype(BF)
            if n == 0:
                go(xa_copy, u, 0)
                go(xa_copy, u, 1)

    def add_far(u):
        for n, row, cols in ((0, x1, slice(0, 1536)), (1, x3, slice(1536, 3072))):
            xa_copy(u, n).wait_recv()
            both = qbuf[u, row, :, cols].astype(F32) + rhalf[u, n].astype(F32)
            qbuf[u, row, :, cols] = both.astype(BF)
            go(xb_copy, u, n)

    def activate(u):
        xb_copy(u, 0).wait_recv()
        xb_copy(u, 1).wait_recv()

        def total(low, width):
            cols = slice(low, low + width)
            mine = qbuf[u, x, :, cols].astype(F32)
            return mine + rfull[u, 0, :, cols].astype(F32) + rfull[u, 1, :, cols].astype(F32)

        def silu_product(low, width):
            gate = total(low, width)
            return (gate / (1.0 + jnp.exp(-gate)) * total(low + width, width)).astype(BF)

        hid[u, c, x, :, 1024:1536] = silu_product(2048, 512)
        hid[u, c, x, :, 0:1024] = silu_product(0, 1024)
        for n in (0, 1):
            go(g_copy, u, n)

        @pl.when(u >= DEEP)
        def _():
            for n in range(3):
                ch_copy(u - DEEP, n, slice(0, 4)).wait_send()

        ch_send(u, x)

    def gather_far(u):
        for n in (0, 1):
            g_copy(u, n).wait_recv()
            go(h_copy, u, n)
        ch_send(u, x3)
        ch_send(u, x1)

    def gather_core(u):
        h_copy(u, 0).wait_recv()
        h_copy(u, 1).wait_recv()
        ch_send(u, x2)

    def multiply_down(u):
        @pl.when(u == 0)
        def _():
            for load in loads[4:]:
                load.wait()

        for n in range(3):
            ch_copy(u, n, slice(0, 4)).wait_recv()
        own = hid[u, :, :, :, 0:1024].reshape(128, 1024)
        mine = hid[u, :, :, :, 1024:1536].reshape(128, 512)
        other = hother[u].reshape(128, 512)
        low = wsd[pl.ds(pl.multiple_of(half * 512, 512), 512), :]
        high = wsd[pl.ds(pl.multiple_of((1 - half) * 512, 512), 512), :]
        spare_sum = jnp.dot(mine, low, preferred_element_type=F32)
        spare_sum = spare_sum + jnp.dot(other, high, preferred_element_type=F32)
        own_out = jnp.dot(own, wd[...], preferred_element_type=F32).astype(BF).reshape(2, 4, 16, 512)
        spare_out = spare_sum.astype(BF).reshape(2, 4, 16, 256)
        for p in (0, 1):
            outs[u, :, p, :, 0:512] = own_out[p]
            outs[u, :, p, :, 512:768] = spare_out[p]
        for n in range(3):
            go(o_copy, u, n)
        back[u, y] = outs[u, y]

    def combine(u):
        for n in range(3):
            o_copy(u, n).wait_recv()
        q = unit_of(u)
        at = pl.ds(pl.multiple_of(half * 256, 256), 256)
        for p in (0, 1):
            block = 2 * q + p
            meta = meta_all[block]
            share = jnp.zeros((8, 128), F32)
            for k in range(8):
                share = share + jnp.where(meta[k:k + 1, :] == back_ids, meta[8 + k:9 + k, :], 0.0)
            spread = jnp.broadcast_to(share[:, None, :], (8, CAP, 128))
            weight = jnp.where(codes(meta, back_ids), spread, 0.0).astype(BF).reshape(128, 128)
            own = back[u, :, p, :, 0:512].reshape(64, 512)
            spare = back[u, :, p, :, 512:768].reshape(64, 256)
            over = (((0,), (0,)), ((), ()))
            dense[block] = lax.dot_general(weight[0:64], own, over, preferred_element_type=F32)
            more = lax.dot_general(weight[64:128], spare, over, preferred_element_type=F32)
            dense[block, :, at] = dense[block, :, at] + more

    def hops(h):
        @pl.when(h == 0)
        def _():
            for d in (0, 1):
                m_copy(d, 0, z_block(d, 0)).start()
            for k in range(PIECES):
                for d in (0, 1):
                    hop_send(d, 0, k)

        @pl.when((h >= 1) & (h <= 7))
        def _():
            for d in (0, 1):
                m_copy(d, h - 1, z_block(d, h)).wait_recv()

            @pl.when(h >= 2)
            def _():
                for d in (0, 1):
                    m_copy(d, h - 2, z_block(d, h - 2)).wait_send()

            m_copy(0, h, z_block(0, h)).start()

            @pl.when(h <= 6)
            def _():
                m_copy(1, h, z_block(1, h)).start()

            for k in range(PIECES):
                for d in (0, 1):
                    hop_wait(d, h - 1, k)

                @pl.when(h >= 2)
                def _():
                    for d in (0, 1):
                        hop_left(d, h - 2, k)

                hop_send(k // (PIECES // 2), h, k)

                @pl.when(h <= 6)
                def _():
                    hop_send(1 - k // (PIECES // 2), h, k)

        @pl.when(h == 8)
        def _():
            m_copy(0, 7, z_block(0, 8)).wait_recv()
            for k in range(PIECES):
                hop_wait(k // (PIECES // 2), 7, k)

    def take(h):
        hops(h)

        @pl.when(h >= 2)
        def _():
            arrive(h - 2)

        select(h)

    def zz_copy(d, j, k):
        rows = slice(PIECE * k, PIECE * k + PIECE)
        at = (d, mod(j, 2), k)
        return rc(
            zsend.at[d, j, rows], zland.at[d, j, rows], zz_s.at[at], zz_r.at[at],
            dev_zm if d == 0 else dev_zp,
        )

    def chain(j, first, second):
        for k in range(PIECES):
            rows = slice(PIECE * k, PIECE * k + PIECE)
            if not first:
                for d in (0, 1):
                    if not (second and k // (PIECES // 2) != d):
                        zz_copy(d, j - 1, k).wait_recv()
            for d in (0, 1):
                if first and k // (PIECES // 2) != d:
                    continue
                block = mod(z + NZ - 8 + j, NZ) if d == 0 else mod(z + 8 - j, NZ)
                value = dense[block, rows]
                if not first and not (second and k // (PIECES // 2) != d):
                    value = value + zland[d, j - 1, rows].astype(F32)
                zsend[d, j, rows] = value.astype(BF)
                if not first and not second:
                    @pl.when((j >= 3) | (k // (PIECES // 2) == d))
                    def _():
                        zz_copy(d, j - 2, k).wait_send()
                zz_copy(d, j, k).start()

    stages = [
        (0, multiply_up), (4, gather_core), (3, gather_far), (1, add_far), (2, activate), (0, add_core),
        (4, multiply_down),
    ]
    late = [(5, combine)]

    def run(t, which):
        for offset, stage in which:
            e = t - offset
            near = (e == 3) | ((e >= 5) & (e <= 7))

            @pl.when(near | ((e >= 9) & (e <= 12)))
            def _():
                stage(jnp.where(e == 3, 0, jnp.where(e <= 7, e - 4, e - 5)))

    def step(t, carry):
        @pl.when(t <= 8)
        def _():
            take(t)

        @pl.when((t == 9) | (t == 10))
        def _():
            arrive(t - 2)

        @pl.when(t == STEPS - 1)
        def _():
            chain(2, False, False)

        run(t, stages)

        run(t, late)

        @pl.when(t == STEPS - 3)
        def _():
            chain(0, True, False)

        @pl.when(t == STEPS - 2)
        def _():
            chain(1, False, True)

        return carry

    lax.fori_loop(0, STEPS, step, 0)

    def chain_step(j, carry):
        chain(j, False, False)
        return carry

    lax.fori_loop(3, 8, chain_step, 0)
    for k in range(PIECES):
        rows = slice(PIECE * k, PIECE * k + PIECE)
        for d in (0, 1):
            zz_copy(d, 7, k).wait_recv()
        value = dense[z, rows] + zland[0, 7, rows].astype(F32) + zland[1, 7, rows].astype(F32)
        out_ref[rows] = value.astype(BF)

    for d, i in ((0, 6), (1, 6), (0, 7)):
        m_copy(d, i, z_block(d, i)).wait_send()
    for k in range(PIECES):
        for d in (0, 1):
            hop_left(d, 6, k)
            zz_copy(d, 6, k).wait_send()
            zz_copy(d, 7, k).wait_send()
        hop_left(k // (PIECES // 2), 7, k)
    for n in range(3):
        for i in range(4):
            y_copy(0, 5 + i, z_block(0, 5 + i), n).wait_send()
            y_copy(1, 4 + i, z_block(1, 4 + i), n).wait_send()
    for u in range(UNITS - DEEP, UNITS):
        c_copy(u, 0).wait_send()
        for n in range(3):
            ch_copy(u, n, slice(0, 4)).wait_send()
            o_copy(u, n).wait_send()
        for copy in (xa_copy, xb_copy, g_copy, h_copy):
            for n in range(2):
                copy(u, n).wait_send()


def on_device(tokens, slot_of, weight_of, gate_up, down_proj, spare_up, spare_down):
    vmem = pl.BlockSpec(memory_space=pltpu.VMEM)
    hbm = pl.BlockSpec(memory_space=pl.ANY)
    dma = pltpu.SemaphoreType.DMA
    return pl.pallas_call(
        kernel,
        out_shape=jax.ShapeDtypeStruct((128, 512), BF),
        in_specs=[vmem, vmem, vmem, hbm, hbm, hbm, hbm],
        out_specs=vmem,
        scratch_shapes=[
            pltpu.VMEM((512, 3072), BF),
            pltpu.VMEM((1024, 512), BF),
            pltpu.VMEM((1024, 256), BF),
            pltpu.VMEM((NZ, 128, 512), BF),
            pltpu.VMEM((NZ, 16, 128), F32),
            pltpu.VMEM((NZ, 128, 512), BF),
            pltpu.VMEM((NZ, NY, 32, 512), BF),
            pltpu.VMEM((UNITS, 2, 4, 16, 3072), BF),
            pltpu.VMEM((UNITS, 4, 16, 3072), BF),
            pltpu.VMEM((UNITS, 4, 16, 3072), BF),
            pltpu.VMEM((UNITS, 2, 16, 1536), BF),
            pltpu.VMEM((UNITS, 2, 16, 3072), BF),
            pltpu.VMEM((UNITS, 2, 4, 16, 1536), BF),
            pltpu.VMEM((UNITS, 2, 4, 16, 512), BF),
            pltpu.VMEM((UNITS, 4, 2, 16, 768), BF),
            pltpu.VMEM((UNITS, 4, 2, 16, 768), BF),
            pltpu.VMEM((NZ, 128, 512), F32),
            pltpu.VMEM((2, 8, 128, 512), BF),
            pltpu.VMEM((2, 8, 128, 512), BF),
            dma((6,)),
            dma((2, 2, PIECES)), dma((2, 2, PIECES)),
            dma((2, 2)), dma((2, 2)),
            dma((2, 4, 3)), dma((2, 4, 3)),
            dma((4,)), dma((4,)),
            dma((4, 2)), dma((4, 2)),
            dma((4, 2)), dma((4, 2)),
            dma((4, 2)), dma((4, 2)),
            dma((4, 2)), dma((4, 2)),
            dma((4, 3)), dma((4, 3)),
            dma((4, 3)), dma((4, 3)),
            dma((2, 2, PIECES)), dma((2, 2, PIECES)),
        ],
        compiler_params=pltpu.CompilerParams(
            collective_id=0, has_side_effects=True, vmem_limit_bytes=58 * 1024 * 1024
        ),
        cost_estimate=pl.CostEstimate(flops=5 * 10**9, bytes_accessed=6 * 10**6, transcendentals=10**5),
    )(tokens, slot_of.T, weight_of.T, gate_up, down_proj, spare_up, spare_down)


def solution(mesh):
    in_specs = (
        P("expert", "dp"),
        P("expert", None),
        P("expert", None),
        P("expert", None, "dp", None),
        P("expert", None, "dp"),
        P("expert", None, "dp", None),
        P("expert", None, "dp"),
    )
    out_specs = P("expert", "dp")
    return jax.shard_map(
        on_device, mesh=mesh, in_specs=in_specs, out_specs=out_specs, check_vma=False
    )
```

```python
import jax
import jax.numpy as jnp
from jax import lax
from jax.experimental import pallas as pl
from jax.experimental.pallas import tpu as pltpu
from jax.sharding import PartitionSpec as P

NX, NY, NZ = 4, 4, 16
CAP = 16
BF = jnp.bfloat16
F32 = jnp.float32
MESH = pl.DeviceIdType.MESH
UNITS = NZ // 2
PARTS = 3 * UNITS
STEPS = PARTS + 19
DEEP = 4
MANY = 8
PIECES = 8
PIECE = 128 // PIECES


def mod(value, n):
    return lax.rem(value, n)


def kernel(
    tok_ref, slot_ref, weight_ref, gate_ref, down_ref, sup_ref, sdown_ref, out_ref,
    wall, wd, wsd, tok_all, meta_all, sel, arr, part, crecv, qbuf, rhalf, rfull, hid, hother, outs,
    back, dense, zsend, zland,
    w_sem, sent, z_r, m_r, y_r, c_r, xa_r, xb_r, g_r, h_r, ch_r, pt_r, o_r, zz_r,
):
    dp = lax.axis_index("dp")
    ex = lax.axis_index("expert")
    x, c = dp // 2, mod(dp, 2)
    y, z = ex // NZ, mod(ex, NZ)
    half = mod(z, 2)
    pair = z // 2
    x1, x2, x3 = mod(x + 1, NX), mod(x + 2, NX), mod(x + 3, NX)
    y1, y2, y3 = mod(y + 1, NY), mod(y + 2, NY), mod(y + 3, NY)
    z1, z3 = mod(z + 1, NZ), mod(z + NZ - 1, NZ)
    dev_xp, dev_xm = (x1 * 2 + c, ex), (x3 * 2 + c, ex)
    dev_c = (x * 2 + (1 - c), ex)
    dev_zp, dev_zm = (dp, y * NZ + z1), (dp, y * NZ + z3)
    mate = y * NZ + pair * 2 + (1 - half)
    dev_pt, dev_ptc = (dp, mate), (x * 2 + (1 - c), mate)
    dev_y = [(dp, row * NZ + z) for row in (y1, y2, y3)]

    def rc(src, dst, kind, rsem, dev):
        return pltpu.make_async_remote_copy(
            src_ref=src, dst_ref=dst, send_sem=sent.at[kind], recv_sem=rsem, device_id=dev, device_id_type=MESH
        )

    def await_all(ref, rsem):
        rc(ref, ref, 0, rsem, dev_c).wait_recv()

    pairs = (
        (sup_ref, 0, slice(0, 512)), (gate_ref, 1, slice(0, 512)), (gate_ref, 2, slice(512, 1024)),
    )
    loads = []
    for ref, n, cols in pairs:
        for g in (0, 1):
            into = wall.at[n, :, 512 * g:512 * g + 512]
            loads.append(pltpu.make_async_copy(ref.at[0, g, :, cols], into, w_sem.at[len(loads)]))
    loads.append(pltpu.make_async_copy(down_ref.at[0], wd, w_sem.at[6]))
    loads.append(pltpu.make_async_copy(sdown_ref.at[0], wsd, w_sem.at[7]))
    for load in loads:
        load.start()

    tok_all[z] = tok_ref[...]
    meta_all[z, 0:8] = slot_ref[...].astype(F32)
    meta_all[z, 8:16] = weight_ref[...]

    barrier = pltpu.get_barrier_semaphore()
    for dev in (dev_xp, dev_xm, dev_c, dev_zp, dev_zm, dev_ptc, *dev_y):
        pl.semaphore_signal(barrier, inc=1, device_id=dev, device_id_type=MESH)
    pl.semaphore_wait(barrier, 9)

    def z_block(d, i):
        return mod(z + NZ - i, NZ) if d == 0 else mod(z + i, NZ)

    def z_copy(d, i, k, block):
        piece = tok_all.at[block, PIECE * k:PIECE * k + PIECE]
        return rc(piece, piece, 0, z_r.at[mod(i, 2), k], dev_zp if d == 0 else dev_zm)

    def m_copy(d, i, block):
        piece = meta_all.at[block]
        return rc(piece, piece, 1, m_r.at[mod(i, 2)], dev_zp if d == 0 else dev_zm)

    def hop_send(d, i, k):
        z_copy(d, i, k, z_block(d, i)).start()

    def hop_wait(i, k, rows):
        await_all(tok_all.at[0, 0:rows], z_r.at[mod(i, 2), k])

    group = lax.broadcasted_iota(jnp.int32, (8, 128), 0)
    tri = (
        lax.broadcasted_iota(jnp.int32, (128, 128), 0) < lax.broadcasted_iota(jnp.int32, (128, 128), 1)
    ).astype(BF)
    place = lax.broadcasted_iota(jnp.int32, (8, CAP, 128), 1).astype(F32)

    def slot_ids(row, spare):
        own = row * NZ + z
        return jnp.where(spare == 1, NY * NZ + own // 2, own).astype(F32)

    send_ids = slot_ids(mod(y + group // 2 + 1, NY), mod(group, 2))
    back_ids = slot_ids(mod(group, 4), group // 4)

    def codes(meta, ids):
        mask = jnp.zeros((8, 128), F32)
        for k in range(8):
            mask = mask + jnp.where(meta[k:k + 1, :] == ids, 1.0, 0.0)
        rank = jnp.dot(mask.astype(BF), tri, preferred_element_type=F32)
        code = jnp.where(mask > 0.5, rank, -1.0)
        return jnp.broadcast_to(code[:, None, :], (8, CAP, 128)) == place

    def y_copy(d, h, block, n):
        at = (d, mod(h, DEEP))
        return rc(sel.at[block, 2 * n:2 * n + 2], arr.at[block, y], 2, y_r.at[at], dev_y[n])

    def select_one(d, h):
        block = z_block(d, h)

        hot = codes(meta_all[block], send_ids)
        pick = jnp.where(hot, 1.0, 0.0).astype(BF).reshape(128, 128)
        rows = jnp.dot(pick, tok_all[block], preferred_element_type=F32).astype(BF)
        sel[block] = rows.reshape(8, CAP, 512)
        for n in range(3):
            y_copy(d, h, block, n).start()
        arr[block, y] = rows[96:128].reshape(2, CAP, 512)

    def select(h):
        select_one(0, h)

        @pl.when((h >= 1) & (h <= 7))
        def _():
            select_one(1, h)

    def arrive(h):
        await_all(sel.at[0, 0:6], y_r.at[0, mod(h, DEEP)])

        @pl.when((h >= 1) & (h <= 7))
        def _():
            await_all(sel.at[0, 0:6], y_r.at[1, mod(h, DEEP)])

    def unit_of(u):
        shift = jnp.int32(0)
        for n, at in enumerate((0, 1, -1, 2, -3, 4, 3, -2)):
            shift = jnp.where(u == n, at, shift)
        return 2 * mod(pair + shift + UNITS, UNITS), 2 * mod(pair - shift + UNITS, UNITS) + 1

    def go(copy, u, n):
        copy(u, n).start()

    def c_copy(w):
        return rc(part.at[w, 1 - c], crecv.at[w], 3, c_r.at[mod(w, MANY)], dev_c)

    def near(n):
        return dev_xp if n == 0 else dev_xm

    def xa_copy(w, n):
        cols = slice(512 * n, 512 * n + 512)
        return rc(qbuf.at[w, x2, :, cols], rhalf.at[w, n], 4, xa_r.at[mod(w, MANY)], near(n))

    def xb_copy(w, n):
        cols = slice(512 * n, 512 * n + 512)
        row = x1 if n == 0 else x3
        return rc(qbuf.at[w, row, :, cols], rfull.at[w, n, :, cols], 5, xb_r.at[mod(w, MANY)], near(n))

    def xd_copy(w, n):
        cols = slice(512 * (1 - n), 512 * (1 - n) + 512)
        row = x1 if n == 0 else x3
        return rc(qbuf.at[w, row, :, cols], rfull.at[w, n, :, cols], 5, xb_r.at[mod(w, MANY)], near(n))

    def g_copy(w, n):
        piece = hid.at[w, c, x]
        return rc(piece, piece, 6, g_r.at[mod(w, MANY)], near(n))

    def h_copy(w, n):
        piece = hid.at[w, c, x3 if n == 0 else x1, :, 256 * n:256 * n + 256]
        return rc(piece, piece, 7, h_r.at[mod(w, MANY)], near(n))

    def ch_copy(w):
        piece = hid.at[w, c]
        return rc(piece, piece, 8, ch_r.at[mod(w // 3, DEEP)], dev_c)

    def pt_copy(u, n):
        return rc(
            hid.at[3 * u, c], hother.at[u, c], 11, pt_r.at[mod(u, DEEP)], dev_pt if n == 0 else dev_ptc
        )

    def ch_send(w):
        @pl.when(mod(w, 3) == 0)
        def _():
            for n in (0, 1):
                pt_copy(w // 3, n).start()

        ch_copy(w).start()

    def o_copy(u, n):
        return rc(outs.at[u, (y1, y2, y3)[n]], back.at[u, y], 9, o_r.at[mod(u, DEEP)], dev_y[n])

    def multiply_up(w):
        u, n = w // 3, mod(w, 3)
        for i in range(3):
            @pl.when(w == i)
            def _():
                loads[2 * i].wait()
                loads[2 * i + 1].wait()

        which = jnp.where(n == 0, 1, 0)
        rows = jnp.concatenate([arr[block, :, which].reshape(64, 512) for block in unit_of(u)], 0)
        for g in (0, 1):
            cols = slice(512 * g, 512 * g + 512)
            made = jnp.dot(rows, wall[n, :, cols], preferred_element_type=F32)
            part[w, :, :, :, cols] = made.astype(BF).reshape(2, 4, 16, 512)
        c_copy(w).start()

    def add_core(w):
        c_copy(w).wait_recv()
        for n, row in enumerate((x2, x1, x3, x)):
            qbuf[w, row] = (part[w, c, row].astype(F32) + crecv[w, row].astype(F32)).astype(BF)
            if n == 0:
                go(xa_copy, w, 0)
                go(xa_copy, w, 1)
            elif n <= 2:
                go(xd_copy, w, n - 1)

    def add_far(w):
        await_all(rhalf.at[w], xa_r.at[mod(w, MANY)])
        for n, row, cols in ((0, x1, slice(0, 512)), (1, x3, slice(512, 1024))):
            both = qbuf[w, row, :, cols].astype(F32) + rhalf[w, n].astype(F32)
            qbuf[w, row, :, cols] = both.astype(BF)
            go(xb_copy, w, n)

    def activate(w):
        await_all(rfull.at[w], xb_r.at[mod(w, MANY)])

        def total(low, width):
            cols = slice(low, low + width)
            mine = qbuf[w, x, :, cols].astype(F32)
            return mine + rfull[w, 0, :, cols].astype(F32) + rfull[w, 1, :, cols].astype(F32)

        gate = total(0, 512)
        hid[w, c, x] = (gate / (1.0 + jnp.exp(-gate)) * total(512, 512)).astype(BF)
        for n in (0, 1):
            go(g_copy, w, n)

    def gather_far(w):
        await_all(hid.at[w, c, 0:2], g_r.at[mod(w, MANY)])
        for n in (0, 1):
            go(h_copy, w, n)

    def gather_core(w):
        await_all(hid.at[w, c, 0], h_r.at[mod(w, MANY)])
        ch_send(w)

    def multiply_down(u):
        @pl.when(u == 0)
        def _():
            for load in loads[6:]:
                load.wait()

        await_all(hother.at[u], pt_r.at[mod(u, DEEP)])
        await_all(hid.at[0:3, 0], ch_r.at[mod(u, DEEP)])
        mine, first, second = [hid[3 * u + n].reshape(128, 512) for n in range(3)]
        other = hother[u].reshape(128, 512)
        low = wsd[pl.ds(pl.multiple_of(half * 512, 512), 512), :]
        high = wsd[pl.ds(pl.multiple_of((1 - half) * 512, 512), 512), :]
        spare_sum = jnp.dot(mine, low, preferred_element_type=F32)
        spare_sum = spare_sum + jnp.dot(other, high, preferred_element_type=F32)
        own_sum = jnp.dot(first, wd[0:512], preferred_element_type=F32)
        own_sum = own_sum + jnp.dot(second, wd[512:1024], preferred_element_type=F32)
        own_out = own_sum.astype(BF).reshape(2, 4, 16, 512)
        spare_out = spare_sum.astype(BF).reshape(2, 4, 16, 256)
        for p in (0, 1):
            outs[u, :, p, :, 0:512] = own_out[p]
            outs[u, :, p, :, 512:768] = spare_out[p]
        for n in range(3):
            go(o_copy, u, n)
        back[u, y] = outs[u, y]

    def combine(u):
        await_all(outs.at[u, 0:3], o_r.at[mod(u, DEEP)])
        at = pl.ds(pl.multiple_of(half * 256, 256), 256)
        for p, block in enumerate(unit_of(u)):
            meta = meta_all[block]
            share = jnp.zeros((8, 128), F32)
            for k in range(8):
                share = share + jnp.where(meta[k:k + 1, :] == back_ids, meta[8 + k:9 + k, :], 0.0)
            spread = jnp.broadcast_to(share[:, None, :], (8, CAP, 128))
            weight = jnp.where(codes(meta, back_ids), spread, 0.0).astype(BF).reshape(128, 128)
            own = back[u, :, p, :, 0:512].reshape(64, 512)
            spare = back[u, :, p, :, 512:768].reshape(64, 256)
            over = (((0,), (0,)), ((), ()))
            dense[block] = lax.dot_general(weight[0:64], own, over, preferred_element_type=F32)
            more = lax.dot_general(weight[64:128], spare, over, preferred_element_type=F32)
            dense[block, :, at] = dense[block, :, at] + more

    def hops(h):
        @pl.when(h == 0)
        def _():
            for d in (0, 1):
                m_copy(d, 0, z_block(d, 0)).start()
            for k in range(PIECES):
                for d in (0, 1):
                    hop_send(d, 0, k)

        @pl.when((h >= 1) & (h <= 7))
        def _():
            await_all(meta_all.at[0:2], m_r.at[mod(h - 1, 2)])
            m_copy(0, h, z_block(0, h)).start()

            @pl.when(h <= 6)
            def _():
                m_copy(1, h, z_block(1, h)).start()

            for k in range(PIECES):
                hop_wait(h - 1, k, 2 * PIECE)

                hop_send(k // (PIECES // 2), h, k)

                @pl.when(h <= 6)
                def _():
                    hop_send(1 - k // (PIECES // 2), h, k)

        @pl.when(h == 8)
        def _():
            await_all(meta_all.at[0], m_r.at[1])
            for k in range(PIECES):
                hop_wait(7, k, PIECE)

    def take(h):
        hops(h)

        @pl.when(h >= 2)
        def _():
            arrive(h - 2)

        select(h)

    def zz_copy(d, j, k):
        rows = slice(PIECE * k, PIECE * k + PIECE)
        return rc(
            zsend.at[d, j, rows], zland.at[d, j, rows], 10, zz_r.at[mod(j, 2), k],
            dev_zm if d == 0 else dev_zp,
        )

    def chain(j, first, second):
        for k in range(PIECES):
            rows = slice(PIECE * k, PIECE * k + PIECE)
            if not first:
                await_all(tok_all.at[0, 0:PIECE if second else 2 * PIECE], zz_r.at[mod(j - 1, 2), k])
            for d in (0, 1):
                if first and k // (PIECES // 2) != d:
                    continue
                block = mod(z + NZ - 8 + j, NZ) if d == 0 else mod(z + 8 - j, NZ)
                value = dense[block, rows]
                if not first and not (second and k // (PIECES // 2) != d):
                    value = value + zland[d, j - 1, rows].astype(F32)
                zsend[d, j, rows] = value.astype(BF)
                zz_copy(d, j, k).start()

    stages = [
        (0, multiply_up), (1, add_core), (3, add_far), (5, activate), (7, gather_far), (9, gather_core),
    ]
    whole_stages = [(10, multiply_down), (13, combine)]

    def entry(t, offset):
        w = t - offset - 6
        return (w >= 0) & (w < PARTS), w

    def step(t, carry):
        @pl.when((t <= 16) & (mod(t, 2) == 0))
        def _():
            take(t // 2)

        @pl.when((t == 18) | (t == 20))
        def _():
            arrive(t // 2 - 2)

        for offset, stage in stages:
            live, w = entry(t, offset)

            @pl.when(live)
            def _():
                stage(w)

        for offset, stage in whole_stages:
            live, w = entry(t, offset)

            @pl.when(live & (mod(w + 3, 3) == 2))
            def _():
                stage(w // 3)

        @pl.when(t == 36)
        def _():
            chain(0, True, False)

        @pl.when(t == 38)
        def _():
            chain(1, False, True)

        @pl.when((t == 40) | (t == 42))
        def _():
            chain(t // 2 - 18, False, False)

        return carry

    lax.fori_loop(0, STEPS, step, 0)

    def chain_step(j, carry):
        chain(j, False, False)
        return carry

    lax.fori_loop(4, 8, chain_step, 0)
    for k in range(PIECES):
        rows = slice(PIECE * k, PIECE * k + PIECE)
        await_all(tok_all.at[0, 0:2 * PIECE], zz_r.at[1, k])
        value = dense[z, rows] + zland[0, 7, rows].astype(F32) + zland[1, 7, rows].astype(F32)
        out_ref[rows] = value.astype(BF)

    whole = (
        tok_all.at[0:15], meta_all.at[0:15], sel.at[0:12], crecv, rhalf, rfull, hid.at[0:6], hid.at[0:3],
        hid.at[0:12], outs.at[0:6], tok_all.at[0:15], hother,
    )
    for kind, ref in enumerate(whole):
        rc(ref, ref, kind, w_sem.at[0], dev_c).wait_send()


def on_device(tokens, slot_of, weight_of, gate_up, down_proj, spare_up, spare_down):
    vmem = pl.BlockSpec(memory_space=pltpu.VMEM)
    hbm = pl.BlockSpec(memory_space=pl.ANY)
    dma = pltpu.SemaphoreType.DMA
    return pl.pallas_call(
        kernel,
        out_shape=jax.ShapeDtypeStruct((128, 512), BF),
        in_specs=[vmem, vmem, vmem, hbm, hbm, hbm, hbm],
        out_specs=vmem,
        scratch_shapes=[
            pltpu.VMEM((3, 512, 1024), BF),
            pltpu.VMEM((1024, 512), BF),
            pltpu.VMEM((1024, 256), BF),
            pltpu.VMEM((NZ, 128, 512), BF),
            pltpu.VMEM((NZ, 16, 128), F32),
            pltpu.VMEM((NZ, 8, CAP, 512), BF),
            pltpu.VMEM((NZ, NY, 2, CAP, 512), BF),
            pltpu.VMEM((PARTS, 2, 4, 16, 1024), BF),
            pltpu.VMEM((PARTS, 4, 16, 1024), BF),
            pltpu.VMEM((PARTS, 4, 16, 1024), BF),
            pltpu.VMEM((PARTS, 2, 16, 512), BF),
            pltpu.VMEM((PARTS, 2, 16, 1024), BF),
            pltpu.VMEM((PARTS, 2, 4, 16, 512), BF),
            pltpu.VMEM((UNITS, 2, 4, 16, 512), BF),
            pltpu.VMEM((UNITS, 4, 2, 16, 768), BF),
            pltpu.VMEM((UNITS, 4, 2, 16, 768), BF),
            pltpu.VMEM((NZ, 128, 512), F32),
            pltpu.VMEM((2, 8, 128, 512), BF),
            pltpu.VMEM((2, 8, 128, 512), BF),
            dma((8,)),
            dma((12,)),
            dma((2, PIECES)),
            dma((2,)),
            dma((2, DEEP)),
            dma((MANY,)), dma((MANY,)), dma((MANY,)),
            dma((MANY,)), dma((MANY,)),
            dma((DEEP,)),
            dma((DEEP,)),
            dma((DEEP,)),
            dma((2, PIECES)),
        ],
        compiler_params=pltpu.CompilerParams(
            collective_id=0, has_side_effects=True, vmem_limit_bytes=58 * 1024 * 1024
        ),
        cost_estimate=pl.CostEstimate(flops=5 * 10**9, bytes_accessed=6 * 10**6, transcendentals=10**5),
    )(tokens, slot_of.T, weight_of.T, gate_up, down_proj, spare_up, spare_down)


def solution(mesh):
    in_specs = (
        P("expert", "dp"),
        P("expert", None),
        P("expert", None),
        P("expert", None, "dp", None),
        P("expert", None, "dp"),
        P("expert", None, "dp", None),
        P("expert", None, "dp"),
    )
    out_specs = P("expert", "dp")
    return jax.shard_map(
        on_device, mesh=mesh, in_specs=in_specs, out_specs=out_specs, check_vma=False
    )
```

```python
import jax
import jax.numpy as jnp
from jax import lax
from jax.experimental import pallas as pl
from jax.experimental.pallas import tpu as pltpu
from jax.sharding import PartitionSpec as P

NX, NY, NZ = 4, 4, 16
CAP = 16
BF = jnp.bfloat16
F32 = jnp.float32
MESH = pl.DeviceIdType.MESH
UNITS = NZ // 2
PARTS = 3 * UNITS
STEPS = PARTS + 18
DEEP = 4
MANY = 8
PIECES = 8
PIECE = 128 // PIECES


def mod(value, n):
    return lax.rem(value, n)


def kernel(
    tok_ref, slot_ref, weight_ref, gate_ref, down_ref, sup_ref, sdown_ref, out_ref,
    wall, wd, wsd, tok_all, meta_all, sel, arr, part, crecv, qbuf, rhalf, rfull, hid, hother, outs,
    back, dense, zsend, zland, slots,
    w_sem, sent, z_r, m_r, y_r, c_r, xa_r, xb_r, g_r, h_r, ch_r, pt_r, o_r, zz_r,
):
    dp = lax.axis_index("dp")
    ex = lax.axis_index("expert")
    x, c = dp // 2, mod(dp, 2)
    y, z = ex // NZ, mod(ex, NZ)
    half = mod(z, 2)
    pair = z // 2
    x1, x2, x3 = mod(x + 1, NX), mod(x + 2, NX), mod(x + 3, NX)
    y1, y2, y3 = mod(y + 1, NY), mod(y + 2, NY), mod(y + 3, NY)
    z1, z3 = mod(z + 1, NZ), mod(z + NZ - 1, NZ)
    dev_xp, dev_xm = (x1 * 2 + c, ex), (x3 * 2 + c, ex)
    dev_c = (x * 2 + (1 - c), ex)
    dev_zp, dev_zm = (dp, y * NZ + z1), (dp, y * NZ + z3)
    mate = y * NZ + pair * 2 + (1 - half)
    dev_pt, dev_ptc = (dp, mate), (x * 2 + (1 - c), mate)
    dev_y = [(dp, row * NZ + z) for row in (y1, y2, y3)]

    def rc(src, dst, kind, rsem, dev):
        return pltpu.make_async_remote_copy(
            src_ref=src, dst_ref=dst, send_sem=sent.at[kind], recv_sem=rsem, device_id=dev, device_id_type=MESH
        )

    def await_all(ref, rsem):
        rc(ref, ref, 0, rsem, dev_c).wait_recv()

    pairs = (
        (sup_ref, 0, slice(0, 512)), (gate_ref, 1, slice(0, 512)), (gate_ref, 2, slice(512, 1024)),
    )
    loads = []
    for ref, n, cols in pairs:
        for g in (0, 1):
            into = wall.at[n, :, 512 * g:512 * g + 512]
            loads.append(pltpu.make_async_copy(ref.at[0, g, :, cols], into, w_sem.at[len(loads)]))
    loads.append(pltpu.make_async_copy(down_ref.at[0], wd, w_sem.at[6]))
    loads.append(pltpu.make_async_copy(sdown_ref.at[0], wsd, w_sem.at[7]))
    firsts = [
        pltpu.make_async_copy(tok_ref, tok_all.at[z], w_sem.at[8]),
        pltpu.make_async_copy(slot_ref, slots, w_sem.at[9]),
        pltpu.make_async_copy(weight_ref, meta_all.at[z, 8:16], w_sem.at[10]),
    ]
    for load in firsts + loads:
        load.start()


    barrier = pltpu.get_barrier_semaphore()
    for dev in (dev_xp, dev_xm, dev_c, dev_zp, dev_zm, dev_ptc, *dev_y):
        pl.semaphore_signal(barrier, inc=1, device_id=dev, device_id_type=MESH)
    for load in firsts:
        load.wait()
    meta_all[z, 0:8] = slots[...].astype(F32)
    pl.semaphore_wait(barrier, 9)

    def z_block(d, i):
        return mod(z + NZ - i, NZ) if d == 0 else mod(z + i, NZ)

    def z_copy(d, i, k, block):
        piece = tok_all.at[block, PIECE * k:PIECE * k + PIECE]
        return rc(piece, piece, 0, z_r.at[mod(i, 2), k], dev_zp if d == 0 else dev_zm)

    def m_copy(d, i, block):
        piece = meta_all.at[block]
        return rc(piece, piece, 1, m_r.at[mod(i, 2)], dev_zp if d == 0 else dev_zm)

    def hop_send(d, i, k):
        z_copy(d, i, k, z_block(d, i)).start()

    def hop_wait(i, k, rows):
        await_all(tok_all.at[0, 0:rows], z_r.at[mod(i, 2), k])

    group = lax.broadcasted_iota(jnp.int32, (8, 128), 0)
    tri = (
        lax.broadcasted_iota(jnp.int32, (128, 128), 0) < lax.broadcasted_iota(jnp.int32, (128, 128), 1)
    ).astype(BF)
    place = lax.broadcasted_iota(jnp.int32, (8, CAP, 128), 1).astype(F32)

    def slot_ids(row, spare):
        own = row * NZ + z
        return jnp.where(spare == 1, NY * NZ + own // 2, own).astype(F32)

    send_ids = slot_ids(mod(y + group // 2 + 1, NY), mod(group, 2))
    back_ids = slot_ids(mod(group, 4), group // 4)

    def codes(meta, ids):
        mask = jnp.zeros((8, 128), F32)
        for k in range(8):
            mask = mask + jnp.where(meta[k:k + 1, :] == ids, 1.0, 0.0)
        rank = jnp.dot(mask.astype(BF), tri, preferred_element_type=F32)
        code = jnp.where(mask > 0.5, rank, -1.0)
        return jnp.broadcast_to(code[:, None, :], (8, CAP, 128)) == place

    def y_copy(d, h, block, n):
        at = (d, mod(h, DEEP))
        return rc(sel.at[block, 2 * n:2 * n + 2], arr.at[block, y], 2, y_r.at[at], dev_y[n])

    def select_one(d, h):
        block = z_block(d, h)

        hot = codes(meta_all[block], send_ids)
        pick = jnp.where(hot, 1.0, 0.0).astype(BF).reshape(128, 128)
        rows = jnp.dot(pick, tok_all[block], preferred_element_type=F32).astype(BF)
        sel[block] = rows.reshape(8, CAP, 512)
        for n in range(3):
            y_copy(d, h, block, n).start()
        arr[block, y] = rows[96:128].reshape(2, CAP, 512)

    def select(h):
        select_one(0, h)

        @pl.when((h >= 1) & (h <= 7))
        def _():
            select_one(1, h)

    def arrive(h):
        await_all(sel.at[0, 0:6], y_r.at[0, mod(h, DEEP)])

        @pl.when((h >= 1) & (h <= 7))
        def _():
            await_all(sel.at[0, 0:6], y_r.at[1, mod(h, DEEP)])

    def unit_of(u):
        shift = jnp.int32(0)
        for n, at in enumerate((0, 1, -1, 2, -3, 4, 3, -2)):
            shift = jnp.where(u == n, at, shift)
        return 2 * mod(pair + shift + UNITS, UNITS), 2 * mod(pair - shift + UNITS, UNITS) + 1

    def go(copy, u, n):
        copy(u, n).start()

    def c_copy(w):
        return rc(part.at[w, 1 - c], crecv.at[w], 3, c_r.at[mod(w, MANY)], dev_c)

    def near(n):
        return dev_xp if n == 0 else dev_xm

    def xa_copy(w, n):
        cols = slice(512 * n, 512 * n + 512)
        return rc(qbuf.at[w, x2, :, cols], rhalf.at[w, n], 4, xa_r.at[mod(w, MANY)], near(n))

    def xb_copy(w, n):
        cols = slice(512 * n, 512 * n + 512)
        row = x1 if n == 0 else x3
        return rc(qbuf.at[w, row, :, cols], rfull.at[w, n, :, cols], 5, xb_r.at[mod(w, MANY)], near(n))

    def xd_copy(w, n):
        cols = slice(512 * (1 - n), 512 * (1 - n) + 512)
        row = x1 if n == 0 else x3
        return rc(qbuf.at[w, row, :, cols], rfull.at[w, n, :, cols], 5, xb_r.at[mod(w, MANY)], near(n))

    def g_copy(w, n):
        piece = hid.at[w, c, x]
        return rc(piece, piece, 6, g_r.at[mod(w, MANY)], near(n))

    def h_copy(w, n):
        piece = hid.at[w, c, x3 if n == 0 else x1, :, 256 * n:256 * n + 256]
        return rc(piece, piece, 7, h_r.at[mod(w, MANY)], near(n))

    def ch_copy(w):
        piece = hid.at[w, c]
        return rc(piece, piece, 8, ch_r.at[mod(w // 3, DEEP)], dev_c)

    def pt_copy(u, n):
        return rc(
            hid.at[3 * u, c], hother.at[u, c], 11, pt_r.at[mod(u, DEEP)], dev_pt if n == 0 else dev_ptc
        )

    def ch_send(w):
        @pl.when(mod(w, 3) == 0)
        def _():
            for n in (0, 1):
                pt_copy(w // 3, n).start()

        ch_copy(w).start()

    def o_copy(u, n):
        return rc(outs.at[u, (y1, y2, y3)[n]], back.at[u, y], 9, o_r.at[mod(u, DEEP)], dev_y[n])

    def multiply_up(w):
        u, n = w // 3, mod(w, 3)
        for i in range(3):
            @pl.when(w == i)
            def _():
                loads[2 * i].wait()
                loads[2 * i + 1].wait()

        which = jnp.where(n == 0, 1, 0)
        rows = jnp.concatenate([arr[block, :, which].reshape(64, 512) for block in unit_of(u)], 0)
        for g in (0, 1):
            cols = slice(512 * g, 512 * g + 512)
            made = jnp.dot(rows, wall[n, :, cols], preferred_element_type=F32)
            part[w, :, :, :, cols] = made.astype(BF).reshape(2, 4, 16, 512)
        c_copy(w).start()

    def add_core(w):
        c_copy(w).wait_recv()
        for n, row in enumerate((x2, x1, x3, x)):
            qbuf[w, row] = (part[w, c, row].astype(F32) + crecv[w, row].astype(F32)).astype(BF)
            if n == 0:
                go(xa_copy, w, 0)
                go(xa_copy, w, 1)
            elif n <= 2:
                go(xd_copy, w, n - 1)

    def add_far(w):
        await_all(rhalf.at[w], xa_r.at[mod(w, MANY)])
        for n, row, cols in ((0, x1, slice(0, 512)), (1, x3, slice(512, 1024))):
            both = qbuf[w, row, :, cols].astype(F32) + rhalf[w, n].astype(F32)
            qbuf[w, row, :, cols] = both.astype(BF)
            go(xb_copy, w, n)

    def activate(w):
        await_all(rfull.at[w], xb_r.at[mod(w, MANY)])

        def total(low, width):
            cols = slice(low, low + width)
            mine = qbuf[w, x, :, cols].astype(F32)
            return mine + rfull[w, 0, :, cols].astype(F32) + rfull[w, 1, :, cols].astype(F32)

        gate = total(0, 512)
        hid[w, c, x] = (gate / (1.0 + jnp.exp(-gate)) * total(512, 512)).astype(BF)
        for n in (0, 1):
            go(g_copy, w, n)

    def gather_far(w):
        await_all(hid.at[w, c, 0:2], g_r.at[mod(w, MANY)])
        for n in (0, 1):
            go(h_copy, w, n)

    def gather_core(w):
        await_all(hid.at[w, c, 0], h_r.at[mod(w, MANY)])
        ch_send(w)

    def multiply_down(u):
        @pl.when(u == 0)
        def _():
            for load in loads[6:]:
                load.wait()

        await_all(hother.at[u], pt_r.at[mod(u, DEEP)])
        await_all(hid.at[0:3, 0], ch_r.at[mod(u, DEEP)])
        mine, first, second = [hid[3 * u + n].reshape(128, 512) for n in range(3)]
        other = hother[u].reshape(128, 512)
        low = wsd[pl.ds(pl.multiple_of(half * 512, 512), 512), :]
        high = wsd[pl.ds(pl.multiple_of((1 - half) * 512, 512), 512), :]
        spare_sum = jnp.dot(mine, low, preferred_element_type=F32)
        spare_sum = spare_sum + jnp.dot(other, high, preferred_element_type=F32)
        own_sum = jnp.dot(first, wd[0:512], preferred_element_type=F32)
        own_sum = own_sum + jnp.dot(second, wd[512:1024], preferred_element_type=F32)
        own_out = own_sum.astype(BF).reshape(2, 4, 16, 512)
        spare_out = spare_sum.astype(BF).reshape(2, 4, 16, 256)
        for p in (0, 1):
            outs[u, :, p, :, 0:512] = own_out[p]
            outs[u, :, p, :, 512:768] = spare_out[p]
        for n in range(3):
            go(o_copy, u, n)
        back[u, y] = outs[u, y]

    def combine(u):
        await_all(outs.at[u, 0:3], o_r.at[mod(u, DEEP)])
        at = pl.ds(pl.multiple_of(half * 256, 256), 256)
        for p, block in enumerate(unit_of(u)):
            meta = meta_all[block]
            share = jnp.zeros((8, 128), F32)
            for k in range(8):
                share = share + jnp.where(meta[k:k + 1, :] == back_ids, meta[8 + k:9 + k, :], 0.0)
            spread = jnp.broadcast_to(share[:, None, :], (8, CAP, 128))
            weight = jnp.where(codes(meta, back_ids), spread, 0.0).astype(BF).reshape(128, 128)
            own = back[u, :, p, :, 0:512].reshape(64, 512)
            spare = back[u, :, p, :, 512:768].reshape(64, 256)
            over = (((0,), (0,)), ((), ()))
            dense[block] = lax.dot_general(weight[0:64], own, over, preferred_element_type=F32)
            more = lax.dot_general(weight[64:128], spare, over, preferred_element_type=F32)
            dense[block, :, at] = dense[block, :, at] + more

    def hops(h):
        @pl.when(h == 0)
        def _():
            for d in (0, 1):
                m_copy(d, 0, z_block(d, 0)).start()
            for k in range(PIECES):
                for d in (0, 1):
                    hop_send(d, 0, k)

        @pl.when((h >= 1) & (h <= 7))
        def _():
            await_all(meta_all.at[0:2], m_r.at[mod(h - 1, 2)])
            m_copy(0, h, z_block(0, h)).start()

            @pl.when(h <= 6)
            def _():
                m_copy(1, h, z_block(1, h)).start()

            for k in range(PIECES):
                hop_wait(h - 1, k, 2 * PIECE)

                hop_send(k // (PIECES // 2), h, k)

                @pl.when(h <= 6)
                def _():
                    hop_send(1 - k // (PIECES // 2), h, k)

        @pl.when(h == 8)
        def _():
            await_all(meta_all.at[0], m_r.at[1])
            for k in range(PIECES):
                hop_wait(7, k, PIECE)

    def take(h):
        hops(h)

        select(h)

    def zz_copy(d, j, k):
        rows = slice(PIECE * k, PIECE * k + PIECE)
        return rc(
            zsend.at[d, j, rows], zland.at[d, j, rows], 10, zz_r.at[mod(j, 2), k],
            dev_zm if d == 0 else dev_zp,
        )

    def chain(j, first, second):
        for k in range(PIECES):
            rows = slice(PIECE * k, PIECE * k + PIECE)
            if not first:
                await_all(tok_all.at[0, 0:PIECE if second else 2 * PIECE], zz_r.at[mod(j - 1, 2), k])
            for d in (0, 1):
                if first and k // (PIECES // 2) != d:
                    continue
                block = mod(z + NZ - 8 + j, NZ) if d == 0 else mod(z + 8 - j, NZ)
                value = dense[block, rows]
                if not first and not (second and k // (PIECES // 2) != d):
                    value = value + zland[d, j - 1, rows].astype(F32)
                zsend[d, j, rows] = value.astype(BF)
                zz_copy(d, j, k).start()

    stages = [
        (0, multiply_up), (1, add_core), (3, add_far), (5, activate), (7, gather_far), (9, gather_core),
    ]
    whole_stages = [(10, multiply_down), (13, combine)]

    def entry(t, offset):
        w = t - offset - 5
        return (w >= 0) & (w < PARTS), w

    def step(t, carry):
        @pl.when((t <= 16) & (mod(t, 2) == 0))
        def _():
            take(t // 2)

        @pl.when((t >= 3) & (t <= 19) & (mod(t, 2) == 1))
        def _():
            arrive(t // 2 - 1)

        for offset, stage in stages:
            live, w = entry(t, offset)

            @pl.when(live)
            def _():
                stage(w)

        for offset, stage in whole_stages:
            live, w = entry(t, offset)

            @pl.when(live & (mod(w + 3, 3) == 2))
            def _():
                stage(w // 3)

        @pl.when(t == 35)
        def _():
            chain(0, True, False)

        @pl.when(t == 37)
        def _():
            chain(1, False, True)

        @pl.when((t == 39) | (t == 41))
        def _():
            chain(t // 2 - 17, False, False)

        return carry

    lax.fori_loop(0, STEPS, step, 0)

    def chain_step(j, carry):
        chain(j, False, False)
        return carry

    lax.fori_loop(4, 8, chain_step, 0)
    for k in range(PIECES):
        rows = slice(PIECE * k, PIECE * k + PIECE)
        await_all(tok_all.at[0, 0:2 * PIECE], zz_r.at[1, k])
        value = dense[z, rows] + zland[0, 7, rows].astype(F32) + zland[1, 7, rows].astype(F32)
        out_ref[rows] = value.astype(BF)

    whole = (
        tok_all.at[0:15], meta_all.at[0:15], sel.at[0:12], crecv, rhalf, rfull, hid.at[0:6], hid.at[0:3],
        hid.at[0:12], outs.at[0:6], tok_all.at[0:15], hother,
    )
    for kind, ref in enumerate(whole):
        rc(ref, ref, kind, w_sem.at[0], dev_c).wait_send()


def on_device(tokens, slot_of, weight_of, gate_up, down_proj, spare_up, spare_down):
    vmem = pl.BlockSpec(memory_space=pltpu.VMEM)
    hbm = pl.BlockSpec(memory_space=pl.ANY)
    dma = pltpu.SemaphoreType.DMA
    return pl.pallas_call(
        kernel,
        out_shape=jax.ShapeDtypeStruct((128, 512), BF),
        in_specs=[hbm, hbm, hbm, hbm, hbm, hbm, hbm],
        out_specs=vmem,
        scratch_shapes=[
            pltpu.VMEM((3, 512, 1024), BF),
            pltpu.VMEM((1024, 512), BF),
            pltpu.VMEM((1024, 256), BF),
            pltpu.VMEM((NZ, 128, 512), BF),
            pltpu.VMEM((NZ, 16, 128), F32),
            pltpu.VMEM((NZ, 8, CAP, 512), BF),
            pltpu.VMEM((NZ, NY, 2, CAP, 512), BF),
            pltpu.VMEM((PARTS, 2, 4, 16, 1024), BF),
            pltpu.VMEM((PARTS, 4, 16, 1024), BF),
            pltpu.VMEM((PARTS, 4, 16, 1024), BF),
            pltpu.VMEM((PARTS, 2, 16, 512), BF),
            pltpu.VMEM((PARTS, 2, 16, 1024), BF),
            pltpu.VMEM((PARTS, 2, 4, 16, 512), BF),
            pltpu.VMEM((UNITS, 2, 4, 16, 512), BF),
            pltpu.VMEM((UNITS, 4, 2, 16, 768), BF),
            pltpu.VMEM((UNITS, 4, 2, 16, 768), BF),
            pltpu.VMEM((NZ, 128, 512), F32),
            pltpu.VMEM((2, 8, 128, 512), BF),
            pltpu.VMEM((2, 8, 128, 512), BF),
            pltpu.VMEM((8, 128), jnp.int32),
            dma((11,)),
            dma((12,)),
            dma((2, PIECES)),
            dma((2,)),
            dma((2, DEEP)),
            dma((MANY,)), dma((MANY,)), dma((MANY,)),
            dma((MANY,)), dma((MANY,)),
            dma((DEEP,)),
            dma((DEEP,)),
            dma((DEEP,)),
            dma((2, PIECES)),
        ],
        compiler_params=pltpu.CompilerParams(
            collective_id=0, has_side_effects=True, vmem_limit_bytes=58 * 1024 * 1024
        ),
        cost_estimate=pl.CostEstimate(flops=5 * 10**9, bytes_accessed=6 * 10**6, transcendentals=10**5),
    )(tokens, slot_of.T, weight_of.T, gate_up, down_proj, spare_up, spare_down)


def solution(mesh):
    in_specs = (
        P("expert", "dp"),
        P("expert", None),
        P("expert", None),
        P("expert", None, "dp", None),
        P("expert", None, "dp"),
        P("expert", None, "dp", None),
        P("expert", None, "dp"),
    )
    out_specs = P("expert", "dp")
    return jax.shard_map(
        on_device, mesh=mesh, in_specs=in_specs, out_specs=out_specs, check_vma=False
    )
```
